256 devices in a mesh: dp: 2 (over x_hi), expert: 4 (over x_lo, core), tensor: 32 (over z, y).
Axes of the slice: x: 4 (x_hi: 2, x_lo: 2; x = x_hi * 2 + x_lo), y: 4, z: 8, core: 2. Of those that a mesh axis runs over, the one named last changes fastest.
Arguments:
- tokens: bfloat16 [1024, 7168], P(('dp', 'expert', 'tensor')), may hold values from -6 to 6
- routes: int32 [1024, 2], P(('dp', 'expert', 'tensor')), may hold values from 0 to 3, all different within a row; in each aligned block of 128 rows (0 to 127, 128 to 255, ...) at most 96 rows name the same one
- route_gates: bfloat16 [1024, 2], P(('dp', 'expert', 'tensor')), may hold values from 0.19921875 to 1
- cotangent: bfloat16 [1024, 7168], P(('dp', 'expert', 'tensor')), may hold values from -6 to 6
- dense_gate: bfloat16 [4864, 7168], P('tensor'), may hold values from -0.0625 to 0.0625
- dense_up: bfloat16 [4864, 7168], P('tensor'), may hold values from -0.0625 to 0.0625
- dense_down: bfloat16 [4864, 7168], P('tensor'), may hold values from -0.078125 to 0.078125
- expert_gate: bfloat16 [4, 4864, 7168], P('expert', 'tensor', 'dp'), may hold values from -0.0625 to 0.0625
- expert_up: bfloat16 [4, 4864, 7168], P('expert', 'tensor', 'dp'), may hold values from -0.0625 to 0.0625
- expert_down: bfloat16 [4, 4864, 7168], P('expert', 'tensor', 'dp'), may hold values from -0.078125 to 0.078125
Outputs:
- mixed: bfloat16 [1024, 7168], P(('dp', 'expert', 'tensor'))
- grad_tokens: bfloat16 [1024, 7168], P(('dp', 'expert', 'tensor'))
- grad_expert_gate: bfloat16 [4, 4864, 7168], P('expert', 'tensor', 'dp')
- grad_expert_up: bfloat16 [4, 4864, 7168], P('expert', 'tensor', 'dp')
- grad_expert_down: bfloat16 [4, 4864, 7168], P('expert', 'tensor', 'dp')
The draws below stay inside these ranges and needn't reach their ends.
Inputs may be any that keep to these rules, and one draw needn't show every extreme that they name: `routes`: in each aligned block of 128 rows (one group) the two experts of a row differ and no expert is named by more than 96 rows; in some block an expert is named by exactly 96 rows.
All inputs are finite; a program needn't handle non-finite values.
Results may differ from the reference program's by a relative error of at most 0.022.
Values may be sent and summed in bfloat16 or wider, within the bound.
No kernel may reach another device: no remote copies, remote signals or barrier semaphores. Data moves between devices by JAX's collectives and lax.ppermute only.
A program may use at most 128 MiB of HBM per device.

```python
import math
import jax
import jax.numpy as jnp
import numpy as np
from jax import lax

D = 7168
FD = 4864
FE = 4864
TOK_DEV = 4
EXPERTS = 4
CAP = 96
TOKENS = 1024
N_DP = 2
N_EXPERT = 4
N_TENSOR = 32


def shard_levels(own_key, shape, shards, smallest, largest):
    gain, own = 1.0, jax.random.fold_in(own_key, 6)
    for axis_at, blocks in shards:
        heights = jnp.exp(jax.random.uniform(jax.random.fold_in(own, axis_at), (blocks,), jnp.float32, smallest / len(shards), largest / len(shards)))
        gain = gain * jnp.repeat(heights, shape[axis_at] // blocks).reshape([-1 if axis == axis_at else 1 for axis in range(len(shape))])
    return gain


def routed_block(rng, own, number, rows, amount, top, most, skew):
    ranking = jax.random.permutation(rng, amount)
    packed, usual = portions_of(amount, rows * top, most, skew, True), portions_of(amount, rows * top, most, skew, False)
    places = jnp.arange(amount)

    def named(sizes, turn):
        used = int((sizes > 0).sum())
        fixed = max(1, used // 4)
        passed = fixed + (places - fixed + turn * (used - fixed)) % max(1, amount - fixed)
        return jnp.zeros((amount,), jnp.int32).at[ranking[jnp.where(places < fixed, places, passed)]].set(jnp.asarray(sizes, jnp.int32))

    sizes = jnp.where(number % 4 == 0, named(packed, number // 4), named(usual, number - number // 4 - 1))
    mixed = jax.random.permutation(jax.random.fold_in(own, 3), amount)
    giver, receiver = mixed[0:amount // 2 * 2:2], mixed[1:amount // 2 * 2:2]
    room = jnp.minimum(sizes[giver] - 1, most - sizes[receiver]) // 2
    room = jnp.where((giver == ranking[0]) | (receiver == ranking[0]) | (sizes[receiver] == 0), 0, jnp.maximum(room, 0))
    passed = jax.random.randint(jax.random.fold_in(own, 4), (amount // 2,), 0, 1 << 20) % (room + 1)
    sizes = sizes.at[giver].add(-passed).at[receiver].add(passed)
    labels = jnp.searchsorted(jnp.cumsum(sizes), jnp.arange(rows * top), side="right").astype(jnp.int32)
    grid = labels.reshape(top, rows).T
    grid = grid[jax.random.permutation(jax.random.fold_in(own, 1), rows)]
    turn = jax.random.randint(jax.random.fold_in(own, 2), (rows, 1), 0, top)
    return jnp.take_along_axis(grid, (jnp.arange(top)[None, :] + turn) % top, axis=1)


def portions_of(amount, total, reach, slope, full):
    loads = [(1 << 20) // math.isqrt(grade ** slope) + 1 for grade in range(1, amount + 1)]
    largest = reach if full else min(reach, max(-(-total // amount), total * loads[0] // sum(loads)))
    least = 1 if total - largest >= amount - 1 else 0
    given, surplus = [largest] + [least] * (amount - 1), total - largest - least * (amount - 1)
    while surplus > 0:
        candidates = [i for i in range(1, amount) if given[i] < largest] or [i for i in range(1, amount) if given[i] < reach]
        pool, budget = sum([loads[i] for i in candidates]), surplus
        for i in candidates:
            extra = min(reach - given[i], max(1, budget * loads[i] // pool), surplus)
            given[i] = given[i] + extra
            surplus = surplus - extra
    return np.array(given)


def gaussian(own_key, shape, width, bound, split=(), kind=jnp.bfloat16):
    values = width * jax.random.normal(own_key, shape, jnp.float32)
    if split:
        values = values * shard_levels(own_key, shape, split, -0.22, 0.18)
    return jnp.clip(values, -bound, bound).astype(kind)


def setup_inputs(seed: int = 0) -> dict:
    arg_keys = jax.random.split(jax.random.key(seed), 11)
    tokens = gaussian(arg_keys[0], (TOKENS, D), 1.0, 6.0, ((0, 256),))
    routes_keys = jax.random.split(jax.random.fold_in(arg_keys[1], 1), TOKENS // (TOK_DEV * N_TENSOR))
    routes_turns = jax.random.permutation(jax.random.fold_in(arg_keys[1], 3), TOKENS // (TOK_DEV * N_TENSOR))
    routes = jax.vmap(lambda own, number: routed_block(jax.random.fold_in(arg_keys[1], 2), own, number, TOK_DEV * N_TENSOR, EXPERTS, 2, CAP, 2))(routes_keys, routes_turns).reshape((TOKENS, 2))
    route_gates = jnp.clip(0.19921875 + 0.80078125 * jax.random.uniform(arg_keys[2], (TOKENS, 2), jnp.float32) ** shard_levels(arg_keys[2], (TOKENS, 2), ((0, 256),), -0.2, 0.2), 0.19921875, 1.0).astype(jnp.bfloat16)
    cotangent = gaussian(arg_keys[3], (TOKENS, D), 1.0, 6.0, ((0, 256),))
    dense_gate = gaussian(arg_keys[4], (FD, D), D ** -0.5, 0.0625, ((0, 32),))
    dense_up = gaussian(arg_keys[5], (FD, D), D ** -0.5, 0.0625, ((0, 32),))
    dense_down = gaussian(arg_keys[6], (FD, D), FD ** -0.5, 0.078125, ((0, 32),))
    expert_gate = gaussian(arg_keys[7], (EXPERTS, FE, D), D ** -0.5, 0.0625, ((0, 4), (1, 32), (2, 2)))
    expert_up = gaussian(arg_keys[8], (EXPERTS, FE, D), D ** -0.5, 0.0625, ((0, 4), (1, 32), (2, 2)))
    expert_down = gaussian(arg_keys[9], (EXPERTS, FE, D), FE ** -0.5, 0.078125, ((0, 4), (1, 32), (2, 2)))
    return dict(tokens=tokens, routes=routes, route_gates=route_gates, cotangent=cotangent, dense_gate=dense_gate, dense_up=dense_up, dense_down=dense_down, expert_gate=expert_gate, expert_up=expert_up, expert_down=expert_down)


def silu_slope(preact):
    sigmoid = jax.nn.sigmoid(preact)
    return sigmoid * (1.0 + preact * (1.0 - sigmoid))


def slot_tables(routed, gated, experts, capacity):
    flat_ids = routed.reshape(-1).astype(jnp.int32)
    member = (flat_ids[:, None] == jnp.arange(experts, dtype=jnp.int32)[None, :]).astype(jnp.int32)
    position = jnp.sum((jnp.cumsum(member, axis=0) - member) * member, axis=1).astype(jnp.int32)
    target = (flat_ids * capacity + position).reshape(-1, 2)
    matches = jnp.arange(experts * capacity, dtype=jnp.int32)[:, None, None] == target[None, :, :]
    dispatch = jnp.sum(matches.astype(jnp.float32), axis=2).astype(jnp.bfloat16)
    weighting = jnp.sum(jnp.where(matches, gated.astype(jnp.float32)[None, :, :], 0.0), axis=2).astype(jnp.bfloat16)
    return dispatch, weighting


def block_sums(dense_terms, expert_terms, mixing):
    parts = N_TENSOR
    dense_items = []
    for activity, weight in dense_terms:
        dense_items.append((activity.reshape(activity.shape[0], parts, -1).transpose(1, 0, 2),
                            weight.reshape(parts, -1, weight.shape[1])))
    expert_items = []
    for activity, weight in expert_terms:
        expert_items.append((activity.reshape(activity.shape[0], activity.shape[1], parts, -1).transpose(2, 0, 1, 3),
                             weight.reshape(weight.shape[0], parts, -1, weight.shape[2]).transpose(1, 0, 2, 3)))
    group_rows = dense_terms[0][0].shape[0]

    def step(total, items):
        dense_now, expert_now = items
        dense_part = jnp.zeros((group_rows, D), jnp.float32)
        for activity, weight in dense_now:
            dense_part = dense_part + jnp.dot(activity, weight, preferred_element_type=jnp.float32)
        expert_part = jnp.zeros((EXPERTS, CAP, D), jnp.float32)
        for activity, weight in expert_now:
            expert_part = expert_part + jnp.einsum("ecf,efd->ecd", activity.astype(jnp.float32), weight.astype(jnp.float32))
        expert_part = expert_part.astype(jnp.bfloat16).reshape(-1, D)
        routed_part = jnp.einsum("sg,sd->gd", mixing.astype(jnp.float32), expert_part.astype(jnp.float32))
        return total + dense_part + routed_part, None

    total, _ = lax.scan(step, jnp.zeros((group_rows, D), jnp.float32), (dense_items, expert_items))
    return total.astype(jnp.bfloat16)


def reference(tokens, routes, route_gates, cotangent, dense_gate, dense_up, dense_down, expert_gate, expert_up, expert_down):
    group_rows = TOK_DEV * N_TENSOR
    groups = TOKENS // group_rows
    mixed_list, grads_list, saved = [], [], []
    for group in range(groups):
        row_start = group * group_rows
        group_tokens = tokens[row_start:row_start + group_rows]
        upstream = cotangent[row_start:row_start + group_rows]
        dispatch, weighting = slot_tables(routes[row_start:row_start + group_rows],
                                          route_gates[row_start:row_start + group_rows], EXPERTS, CAP)
        slot_tokens = jnp.dot(dispatch, group_tokens, preferred_element_type=jnp.float32).astype(jnp.bfloat16).reshape(EXPERTS, CAP, D)
        slot_grads = jnp.dot(weighting, upstream, preferred_element_type=jnp.float32).astype(jnp.bfloat16).reshape(EXPERTS, CAP, D)
        expert_pre = jnp.stack([jnp.dot(slot_tokens[index], expert_gate[index].T, preferred_element_type=jnp.float32) for index in range(EXPERTS)])
        expert_lin = jnp.stack([jnp.dot(slot_tokens[index], expert_up[index].T, preferred_element_type=jnp.float32) for index in range(EXPERTS)])
        expert_act = (jax.nn.silu(expert_pre) * expert_lin).astype(jnp.bfloat16)
        expert_dact = jnp.stack([jnp.dot(slot_grads[index], expert_down[index].T, preferred_element_type=jnp.float32) for index in range(EXPERTS)])
        gate_grad = (expert_dact * expert_lin * silu_slope(expert_pre)).astype(jnp.bfloat16)
        lin_grad = (expert_dact * jax.nn.silu(expert_pre)).astype(jnp.bfloat16)
        dense_pre = jnp.dot(group_tokens, dense_gate.T, preferred_element_type=jnp.float32)
        dense_lin = jnp.dot(group_tokens, dense_up.T, preferred_element_type=jnp.float32)
        dense_act = (jax.nn.silu(dense_pre) * dense_lin).astype(jnp.bfloat16)
        dense_dact = jnp.dot(upstream, dense_down.T, preferred_element_type=jnp.float32)
        dense_gate_grad = (dense_dact * dense_lin * silu_slope(dense_pre)).astype(jnp.bfloat16)
        dense_lin_grad = (dense_dact * jax.nn.silu(dense_pre)).astype(jnp.bfloat16)
        mixed_list.append(block_sums([(dense_act, dense_down)], [(expert_act, expert_down)], weighting))
        grads_list.append(block_sums([(dense_gate_grad, dense_gate), (dense_lin_grad, dense_up)],
                                     [(gate_grad, expert_gate), (lin_grad, expert_up)], dispatch))
        saved.append((slot_tokens, slot_grads, expert_act, gate_grad, lin_grad))
    stacks = [jnp.stack(list(column)) for column in zip(*saved)]
    grad_gate, grad_up, grad_down = [], [], []
    for index in range(EXPERTS):
        gate_total = jnp.zeros((FE, D), jnp.float32)
        up_total = jnp.zeros((FE, D), jnp.float32)
        down_total = jnp.zeros((FE, D), jnp.float32)
        for data_index in range(N_DP):
            chosen = slice(data_index * N_EXPERT, (data_index + 1) * N_EXPERT)
            slot_rows = stacks[0][chosen, index].reshape(-1, D)
            grad_rows = stacks[1][chosen, index].reshape(-1, D)
            act_rows = stacks[2][chosen, index].reshape(-1, FE)
            gate_rows = stacks[3][chosen, index].reshape(-1, FE)
            lin_rows = stacks[4][chosen, index].reshape(-1, FE)
            part_gate = lax.optimization_barrier(jnp.dot(gate_rows.T, slot_rows, preferred_element_type=jnp.float32).astype(jnp.bfloat16))
            part_up = lax.optimization_barrier(jnp.dot(lin_rows.T, slot_rows, preferred_element_type=jnp.float32).astype(jnp.bfloat16))
            part_down = lax.optimization_barrier(jnp.dot(act_rows.T, grad_rows, preferred_element_type=jnp.float32).astype(jnp.bfloat16))
            gate_total = gate_total + part_gate.astype(jnp.float32)
            up_total = up_total + part_up.astype(jnp.float32)
            down_total = down_total + part_down.astype(jnp.float32)
        grad_gate.append(gate_total.astype(jnp.bfloat16))
        grad_up.append(up_total.astype(jnp.bfloat16))
        grad_down.append(down_total.astype(jnp.bfloat16))
    return (jnp.concatenate(mixed_list, axis=0), jnp.concatenate(grads_list, axis=0),
            jnp.stack(grad_gate), jnp.stack(grad_up), jnp.stack(grad_down))
```

```python
import jax
import jax.numpy as jnp
from jax import lax
from jax.sharding import Mesh, PartitionSpec as P

BF = jnp.bfloat16
F32 = jnp.float32
ZMODE = "pp"


def shift(value, axis, by):
    size = lax.axis_size(axis)
    return lax.ppermute(value, axis, [(i, (i + by) % size) for i in range(size)])


def swap(value, axes):
    size = 1
    for axis in axes:
        size *= lax.axis_size(axis)
    return lax.ppermute(value, axes, [(i, size - 1 - i) for i in range(size)])


def z_steps(size):
    order = []
    for step in range(1, (size + 1) // 2):
        order += [step, -step]
    return order + [size // 2]


def gather_z(block):
    size = lax.axis_size("z")
    if ZMODE == "pp":
        return jnp.concatenate([block] + [shift(block, "z", -by) for by in z_steps(size)], axis=0)
    if ZMODE == "a2a":
        wide = jnp.broadcast_to(block[None], (size,) + block.shape)
        return lax.all_to_all(wide, "z", 0, 0, tiled=True).reshape(-1, block.shape[1])
    return lax.all_gather(block, "z", axis=0, tiled=True)


def scatter_z(part):
    size = lax.axis_size("z")
    rows = part.shape[0] // size
    if ZMODE == "pp":
        pieces = [part[i * rows:(i + 1) * rows] for i in range(size)]
        total = pieces[0].astype(F32)
        for by, piece in zip(z_steps(size), pieces[1:]):
            total = total + shift(piece, "z", by).astype(F32)
        return total
    landed = lax.all_to_all(part.reshape(size, rows, -1), "z", 0, 0, tiled=True)
    return jnp.sum(landed.astype(F32), axis=0)


def gather_y(block):
    half = block.shape[0] // 2
    before = shift(block, "y", 1)
    after = shift(block, "y", -1)
    far = jnp.concatenate([shift(before[:half], "y", 1), shift(after[half:], "y", -1)], axis=0)
    return jnp.concatenate([block, before, after, far], axis=0)


def scatter_y(part):
    rows = part.shape[0] // 4
    half = rows // 2
    own, before, after, far = [part[i * rows:(i + 1) * rows] for i in range(4)]
    first = shift(far[:half], "y", -1)
    second = shift(far[half:], "y", 1)
    before = jnp.concatenate([(before[:half].astype(F32) + first.astype(F32)).astype(BF), before[half:]], axis=0)
    after = jnp.concatenate([after[:half], (after[half:].astype(F32) + second.astype(F32)).astype(BF)], axis=0)
    return (own.astype(F32) + shift(before, "y", -1).astype(F32) + shift(after, "y", 1).astype(F32)).astype(BF)


def in_order(data, mine, other):
    return jnp.where(data == 0, jnp.concatenate([mine, other], axis=0), jnp.concatenate([other, mine], axis=0))


def spread(mine, other, data):
    return jnp.concatenate(
        [
            in_order(data, mine, swap(other, ("dp",))),
            in_order(data, swap(mine, ("xlo",)), swap(other, ("dp", "xlo"))),
        ],
        axis=0,
    )


def finish(part, data):
    rows = part.shape[0] // 4
    first, second, third, fourth = [part[i * rows:(i + 1) * rows] for i in range(4)]
    own, by_dp = jnp.where(data == 0, first, second), jnp.where(data == 0, second, first)
    by_x, by_both = jnp.where(data == 0, third, fourth), jnp.where(data == 0, fourth, third)
    mine = own + swap(by_x, ("xlo",))
    other = swap(by_dp, ("dp",)) + swap(by_both, ("dp", "xlo"))
    return jnp.where(
        data == 0, jnp.concatenate([mine, other], axis=1), jnp.concatenate([other, mine], axis=1)
    ).astype(BF)


def dot(left, right, dims):
    return lax.dot_general(left, right, (dims, ((), ())), preferred_element_type=F32)


def per_device(
    tokens, routes, route_gates, cotangent, dense_gate, dense_up, dense_down,
    expert_gate, expert_up, expert_down,
):
    width = expert_gate.shape[2]
    hidden = expert_gate.shape[1]
    hidden_half = hidden // 2
    data, near, core = (lax.axis_index(name) for name in ("dp", "xlo", "core"))
    experts = lax.axis_size("xlo") * lax.axis_size("core")
    rows = tokens.shape[0]

    def columns(array, at):
        return lax.dynamic_slice_in_dim(array, at * width, width, axis=1)

    ids = jnp.arange(128, dtype=jnp.int32)
    weights_of = jnp.sum(
        jnp.where(routes[:, :, None] == ids[None, None, :], route_gates.astype(F32)[:, :, None], 0.0), axis=1
    ).astype(BF)
    tok = spread(
        jnp.concatenate([columns(tokens, data), weights_of], axis=1),
        jnp.concatenate([columns(tokens, 1 - data), weights_of], axis=1),
        data,
    )
    cot = spread(columns(cotangent, data), columns(cotangent, 1 - data), data)
    tok = gather_y(gather_z(tok))
    cot = gather_y(gather_z(cot))

    expert_mine = jnp.stack([expert_gate[0], expert_up[0], expert_down[0]])
    expert_other = swap(expert_mine, ("core",))

    def pack(at, dense):
        dense_part = lax.dynamic_slice(dense, (near * hidden_half, data * width), (hidden_half, width))
        return jnp.concatenate([expert_mine[at], expert_other[at], dense_part], axis=0)

    gate, up, down = pack(0, dense_gate), pack(1, dense_up), pack(2, dense_down)

    weighting = tok[:, width:].astype(F32)
    tok = tok[:, :width]
    expert_id = near * lax.axis_size("core") + core
    mine_w = jnp.sum(jnp.where(ids[None] == expert_id, weighting, 0.0), axis=1, keepdims=True)
    other_w = jnp.sum(jnp.where(ids[None] == expert_id + 1 - 2 * core, weighting, 0.0), axis=1, keepdims=True)
    unit = jnp.arange(2 * hidden + hidden_half, dtype=jnp.int32)[None]
    scale = jnp.where(unit < hidden, mine_w, jnp.where(unit < 2 * hidden, other_w, 1.0))

    pre = dot(tok, gate, ((1,), (1,))).astype(BF)
    lin = dot(tok, up, ((1,), (1,))).astype(BF)
    dact = dot(cot, down, ((1,), (1,))).astype(BF)

    def both(value):
        return value.astype(F32) + swap(value, ("dp",)).astype(F32)

    pre, lin, dact = both(pre), both(lin), both(dact) * scale
    sig = jax.nn.sigmoid(pre)
    act = (pre * sig * lin * scale).astype(BF)
    gate_grad = (dact * lin * (sig * (1.0 + pre * (1.0 - sig)))).astype(BF)
    lin_grad = (dact * (pre * sig)).astype(BF)

    mixed = dot(act, down, ((1,), (0,))).astype(BF)
    mixed = finish(scatter_z(scatter_y(mixed)), data)
    grads = (dot(gate_grad, gate, ((1,), (0,))) + dot(lin_grad, up, ((1,), (0,)))).astype(BF)
    grads = finish(scatter_z(scatter_y(grads)), data)

    def weight_grad(left, right):
        term = dot(left[:, :2 * hidden], right, ((0,), (0,))).astype(BF)
        return (term[:hidden].astype(F32) + swap(term[hidden:], ("core",)).astype(F32)).astype(BF)[None]

    return (mixed, grads, weight_grad(gate_grad, tok), weight_grad(lin_grad, tok), weight_grad(act, cot))


def solution(mesh):
    fine = Mesh(mesh.devices.reshape(2, 2, 2, 8, 4), ("dp", "xlo", "core", "z", "y"))
    every = ("dp", "xlo", "core", "z", "y")
    row = P(every, None)
    dense = P(("z", "y"), None)
    expert = P(("xlo", "core"), ("z", "y"), "dp")
    return jax.shard_map(
        per_device,
        mesh=fine,
        in_specs=(row, row, row, row, dense, dense, dense, expert, expert, expert),
        out_specs=(row, row, expert, expert, expert),
        check_vma=False,
    )
```

```python
import jax
import jax.numpy as jnp
from jax import lax
from jax.sharding import Mesh, PartitionSpec as P

BF = jnp.bfloat16
F32 = jnp.float32


def shift(value, axis, by):
    size = lax.axis_size(axis)
    return lax.ppermute(value, axis, [(i, (i + by) % size) for i in range(size)])


def swap(value, axes):
    size = 1
    for axis in axes:
        size *= lax.axis_size(axis)
    return lax.ppermute(value, axes, [(i, size - 1 - i) for i in range(size)])


def gather(block, axis):
    size = lax.axis_size(axis)
    wide = jnp.broadcast_to(block[None], (size,) + block.shape)
    return lax.all_to_all(wide, axis, 0, 0, tiled=True).reshape(-1, block.shape[1])


def scatter(part, axis):
    size = lax.axis_size(axis)
    landed = lax.all_to_all(part.reshape(size, -1, part.shape[1]), axis, 0, 0, tiled=True)
    return jnp.sum(landed.astype(F32), axis=0)


def in_order(data, mine, other):
    return jnp.where(data == 0, jnp.concatenate([mine, other], axis=0), jnp.concatenate([other, mine], axis=0))


def finish(part, data):
    rows = part.shape[0] // 2
    own = jnp.where(data == 0, part[:rows], part[rows:])
    other = swap(jnp.where(data == 0, part[rows:], part[:rows]), ("dp",))
    return jnp.where(
        data == 0, jnp.concatenate([own, other], axis=1), jnp.concatenate([other, own], axis=1)
    ).astype(BF)


def dot(left, right, dims):
    return lax.dot_general(left, right, (dims, ((), ())), preferred_element_type=F32)


def per_device(
    tokens, routes, route_gates, cotangent, dense_gate, dense_up, dense_down,
    expert_gate, expert_up, expert_down,
):
    width = expert_gate.shape[2]
    hidden = expert_gate.shape[1]
    hidden_half = hidden // 2
    data, near, core = (lax.axis_index(name) for name in ("dp", "xlo", "core"))
    experts = lax.axis_size("xlo") * lax.axis_size("core")
    rows = tokens.shape[0]

    def columns(array, at):
        return lax.dynamic_slice_in_dim(array, at * width, width, axis=1)

    ids = jnp.arange(128, dtype=jnp.int32)
    weights_of = jnp.sum(
        jnp.where(routes[:, :, None] == ids[None, None, :], route_gates.astype(F32)[:, :, None], 0.0), axis=1
    ).astype(BF)
    tok_own = jnp.concatenate([columns(tokens, data), weights_of], axis=1)
    tok_far = jnp.concatenate([columns(tokens, 1 - data), weights_of], axis=1)
    cot = in_order(data, columns(cotangent, data), swap(columns(cotangent, 1 - data), ("dp",)))
    cot = gather(gather(cot, "z"), "y")
    cots = (cot, swap(cot, ("xlo",)))
    tok = jnp.concatenate(
        [
            in_order(data, tok_own, swap(tok_far, ("dp",))),
            in_order(data, swap(tok_own, ("xlo",)), swap(tok_far, ("dp", "xlo"))),
        ],
        axis=0,
    )
    pair = tok.shape[0] // 2
    tok = gather(tok, "z").reshape(-1, 2, pair, tok.shape[1])
    toks = [gather(tok[:, q].reshape(-1, tok.shape[3]), "y") for q in range(2)]

    expert_mine = jnp.stack([expert_gate[0], expert_up[0], expert_down[0]])
    expert_other = swap(expert_mine, ("core",))
    units = -(-(2 * hidden + hidden_half) // 128) * 128
    spare = jnp.zeros((units - 2 * hidden - hidden_half, width), BF)

    def pack(at, dense):
        dense_part = lax.dynamic_slice(dense, (near * hidden_half, data * width), (hidden_half, width))
        return [expert_mine[at], expert_other[at], dense_part, spare]

    gate_up = jnp.concatenate(pack(0, dense_gate) + pack(1, dense_up), axis=0)
    down = jnp.concatenate(pack(2, dense_down), axis=0)

    unit = jnp.arange(units, dtype=jnp.int32)[None]
    expert_id = near * lax.axis_size("core") + core
    terms = []
    for tok, cot in zip(toks, cots):
        weighting = tok[:, width:].astype(F32)
        tok = tok[:, :width]
        mine_w = jnp.sum(jnp.where(ids[None] == expert_id, weighting, 0.0), axis=1, keepdims=True)
        other_w = jnp.sum(jnp.where(ids[None] == expert_id + 1 - 2 * core, weighting, 0.0), axis=1, keepdims=True)
        scale = jnp.where(unit < hidden, mine_w, jnp.where(unit < 2 * hidden, other_w, 1.0))
        both = dot(tok, gate_up, ((1,), (1,))).astype(BF)
        both = both.astype(F32) + swap(both, ("dp",)).astype(F32)
        pre, lin = both[:, :units], both[:, units:]
        dact = dot(cot, down, ((1,), (1,))).astype(BF)
        dact = (dact.astype(F32) + swap(dact, ("dp",)).astype(F32)) * scale
        sig = jax.nn.sigmoid(pre)
        act = (pre * sig * lin * scale).astype(BF)
        gate_grad = (dact * lin * (sig * (1.0 + pre * (1.0 - sig)))).astype(BF)
        lin_grad = (dact * (pre * sig)).astype(BF)
        terms.append((tok, cot, act, gate_grad, lin_grad))

    mixed, grads = [], []
    for tok, cot, act, gate_grad, lin_grad in terms:
        both = jnp.concatenate([gate_grad, lin_grad], axis=1)
        grads.append(dot(both, gate_up, ((1,), (0,))).astype(BF))
        mixed.append(scatter(dot(act, down, ((1,), (0,))).astype(BF), "y").astype(BF))

    depth = lax.axis_size("z")
    mixed = jnp.concatenate([part.reshape(depth, pair, width) for part in mixed], axis=1)
    mixed = scatter(mixed.reshape(-1, width), "z")
    mixed = finish(mixed[:pair] + swap(mixed[pair:], ("xlo",)), data)

    grads = (grads[0].astype(F32) + swap(grads[1], ("xlo",)).astype(F32)).astype(BF)
    grads = finish(scatter(scatter(grads, "y").astype(BF), "z"), data)

    def weight_grad(lefts, rights):
        term = dot(lefts[0][:, :2 * hidden], rights[0], ((0,), (0,)))
        term = (term + dot(lefts[1][:, :2 * hidden], rights[1], ((0,), (0,)))).astype(BF)
        return (term[:hidden].astype(F32) + swap(term[hidden:], ("core",)).astype(F32)).astype(BF)[None]

    tok, cot, act, gate_grad, lin_grad = zip(*terms)
    return (
        mixed,
        grads,
        weight_grad(gate_grad, tok),
        weight_grad(lin_grad, tok),
        weight_grad(act, cot),
    )


def solution(mesh):
    fine = Mesh(mesh.devices.reshape(2, 2, 2, 8, 4), ("dp", "xlo", "core", "z", "y"))
    every = ("dp", "xlo", "core", "z", "y")
    row = P(every, None)
    dense = P(("z", "y"), None)
    expert = P(("xlo", "core"), ("z", "y"), "dp")
    return jax.shard_map(
        per_device,
        mesh=fine,
        in_specs=(row, row, row, row, dense, dense, dense, expert, expert, expert),
        out_specs=(row, row, expert, expert, expert),
        check_vma=False,
    )
```

```python
import jax
import jax.numpy as jnp
from jax import lax
from jax.sharding import Mesh, PartitionSpec as P

BF = jnp.bfloat16
F32 = jnp.float32


def shift(value, axis, by):
    size = lax.axis_size(axis)
    return lax.ppermute(value, axis, [(i, (i + by) % size) for i in range(size)])


def swap(value, axes):
    size = 1
    for axis in axes:
        size *= lax.axis_size(axis)
    return lax.ppermute(value, axes, [(i, size - 1 - i) for i in range(size)])


def scatter(part, axis):
    size = lax.axis_size(axis)
    landed = lax.all_to_all(part.reshape(size, -1, part.shape[1]), axis, 0, 0, tiled=True)
    return jnp.sum(landed.astype(F32), axis=0)


def in_order(data, mine, other):
    return jnp.where(data == 0, jnp.concatenate([mine, other], axis=0), jnp.concatenate([other, mine], axis=0))


def join(parts):
    return jnp.concatenate(parts, axis=0)


def gather_y(block):
    half = block.shape[0] // 2
    before = shift(block, "y", 1)
    after = shift(block, "y", -1)
    return [block, before, after, join([shift(before[:half], "y", 1), shift(after[half:], "y", -1)])]


def scatter_y(parts):
    own, before, after, far = parts
    half = far.shape[0] // 2
    first = shift(far[:half], "y", -1).astype(F32)
    second = shift(far[half:], "y", 1).astype(F32)
    none = jnp.zeros_like(first)
    before = (before.astype(F32) + join([first, none])).astype(BF)
    after = (after.astype(F32) + join([none, second])).astype(BF)
    return (own.astype(F32) + shift(before, "y", -1).astype(F32) + shift(after, "y", 1).astype(F32)).astype(BF)


def finish(part, data):
    rows = part.shape[0] // 2
    own = jnp.where(data == 0, part[:rows], part[rows:])
    other = swap(jnp.where(data == 0, part[rows:], part[:rows]), ("dp",))
    return jnp.where(
        data == 0, jnp.concatenate([own, other], axis=1), jnp.concatenate([other, own], axis=1)
    ).astype(BF)


def dot(left, right, dims):
    return lax.dot_general(left, right, (dims, ((), ())), preferred_element_type=F32)


def per_device(
    tokens, routes, route_gates, cotangent, dense_gate, dense_up, dense_down,
    expert_gate, expert_up, expert_down,
):
    width = expert_gate.shape[2]
    hidden = expert_gate.shape[1]
    hidden_half = hidden // 2
    data, near, core = (lax.axis_index(name) for name in ("dp", "xlo", "core"))
    experts = lax.axis_size("xlo") * lax.axis_size("core")
    rows = tokens.shape[0]

    def columns(array, at):
        return lax.dynamic_slice_in_dim(array, at * width, width, axis=1)

    ids = jnp.arange(128, dtype=jnp.int32)
    weights_of = jnp.sum(
        jnp.where(routes[:, :, None] == ids[None, None, :], route_gates.astype(F32)[:, :, None], 0.0), axis=1
    ).astype(BF)
    rows = tokens.shape[0]
    blank = jnp.zeros_like(weights_of)
    tok_own = jnp.concatenate([columns(tokens, data), weights_of], axis=1)
    tok_far = jnp.concatenate([columns(tokens, 1 - data), weights_of], axis=1)
    cot_own = jnp.concatenate([columns(cotangent, data), blank], axis=1)
    cot_far = jnp.concatenate([columns(cotangent, 1 - data), blank], axis=1)
    by_dp = swap(join([tok_far, cot_far]), ("dp",))
    by_x = swap(tok_own, ("xlo",))
    by_both = swap(tok_far, ("dp", "xlo"))
    block = join(
        [in_order(data, tok_own, by_dp[:rows]), in_order(data, by_x, by_both), in_order(data, cot_own, by_dp[rows:])]
    )
    depth = lax.axis_size("z")
    block = lax.all_gather(block, "z", axis=0, tiled=True).reshape(depth, 3, 2 * rows, -1)

    expert_mine = jnp.stack([expert_gate[0], expert_up[0], expert_down[0]])
    expert_other = swap(expert_mine, ("core",))
    units = -(-(2 * hidden + hidden_half) // 128) * 128

    def pack(at, dense):
        dense_part = lax.dynamic_slice(dense, (near * hidden_half, data * width), (hidden_half, width))
        return sum(
            lax.pad(part, jnp.zeros((), BF), ((start, units - start - part.shape[0], 0), (0, 0, 0)))
            for start, part in ((0, expert_mine[at]), (hidden, expert_other[at]), (2 * hidden, dense_part))
        )

    gate_up = join([pack(0, dense_gate), pack(1, dense_up)])
    down = pack(2, dense_down)
    block, gate_up, down = lax.optimization_barrier((block, gate_up, down))

    toks = gather_y(block[:, :2].transpose(1, 0, 2, 3).reshape(-1, block.shape[3]))
    cots = gather_y(block[:, 2, :, :width].reshape(-1, width))
    cots = [join([cot, swap(cot, ("xlo",))]) for cot in cots]

    unit = jnp.arange(units, dtype=jnp.int32)[None]
    expert_id = near * lax.axis_size("core") + core
    terms = []
    for tok, cot in zip(toks, cots):
        weighting = tok[:, width:].astype(F32)
        tok = tok[:, :width]
        mine_w = jnp.sum(jnp.where(ids[None] == expert_id, weighting, 0.0), axis=1, keepdims=True)
        other_w = jnp.sum(jnp.where(ids[None] == expert_id + 1 - 2 * core, weighting, 0.0), axis=1, keepdims=True)
        scale = jnp.where(unit < hidden, mine_w, jnp.where(unit < 2 * hidden, other_w, 1.0))
        both = dot(tok, gate_up, ((1,), (1,))).astype(BF)
        both = both.astype(F32) + swap(both, ("dp",)).astype(F32)
        pre, lin = both[:, :units], both[:, units:]
        dact = dot(cot, down, ((1,), (1,))).astype(BF)
        dact = (dact.astype(F32) + swap(dact, ("dp",)).astype(F32)) * scale
        sig = jax.nn.sigmoid(pre)
        act = (pre * sig * lin * scale).astype(BF)
        gate_grad = (dact * lin * (sig * (1.0 + pre * (1.0 - sig)))).astype(BF)
        lin_grad = (dact * (pre * sig)).astype(BF)
        terms.append((tok, cot, act, gate_grad, lin_grad))

    mixed = [dot(act, down, ((1,), (0,))).astype(BF) for _, _, act, _, _ in terms]
    grads = [
        dot(jnp.concatenate([gate_grad, lin_grad], axis=1), gate_up, ((1,), (0,)))
        for _, _, _, gate_grad, lin_grad in terms
    ]
    mixed, grads, terms = lax.optimization_barrier((mixed, grads, terms))

    half = grads[0].shape[0] // 2
    grads = [(part[:half] + swap(part[half:].astype(BF), ("xlo",)).astype(F32)).astype(BF) for part in grads]
    grads = scatter_y(grads)

    mixed = scatter_y(mixed).reshape(2, depth, 2 * rows, width).transpose(1, 0, 2, 3).reshape(-1, width)
    mixed = scatter(mixed, "z")
    mixed = finish(mixed[:2 * rows] + swap(mixed[2 * rows:], ("xlo",)), data)
    grads = finish(scatter(grads, "z"), data)

    def weight_grad(left, right):
        term = dot(left[:, :2 * hidden], right, ((0,), (0,))).astype(BF)
        return (term[:hidden].astype(F32) + swap(term[hidden:], ("core",)).astype(F32)).astype(BF)[None]

    tok, cot, act, gate_grad, lin_grad = [join(parts) for parts in zip(*terms)]
    return (
        mixed,
        grads,
        weight_grad(gate_grad, tok),
        weight_grad(lin_grad, tok),
        weight_grad(act, cot),
    )


def solution(mesh):
    fine = Mesh(mesh.devices.reshape(2, 2, 2, 8, 4), ("dp", "xlo", "core", "z", "y"))
    every = ("dp", "xlo", "core", "z", "y")
    row = P(every, None)
    dense = P(("z", "y"), None)
    expert = P(("xlo", "core"), ("z", "y"), "dp")
    return jax.shard_map(
        per_device,
        mesh=fine,
        in_specs=(row, row, row, row, dense, dense, dense, expert, expert, expert),
        out_specs=(row, row, expert, expert, expert),
        check_vma=False,
    )
```

```python
import jax
import jax.numpy as jnp
from jax import lax
from jax.sharding import Mesh, PartitionSpec as P

BF = jnp.bfloat16
F32 = jnp.float32


def swap(value, axes):
    size = 1
    for axis in axes:
        size *= lax.axis_size(axis)
    return lax.ppermute(value, axes, [(i, size - 1 - i) for i in range(size)])


def scatter(part, axis):
    size = lax.axis_size(axis)
    landed = lax.all_to_all(part.reshape(size, -1, part.shape[1]), axis, 0, 0, tiled=True)
    return jnp.sum(landed.astype(F32), axis=0)


def in_order(data, mine, other):
    return jnp.where(data == 0, jnp.concatenate([mine, other], axis=0), jnp.concatenate([other, mine], axis=0))


def gather(block, axis):
    size = lax.axis_size(axis)
    wide = jnp.broadcast_to(block[None], (size,) + block.shape)
    return lax.all_to_all(wide, axis, 0, 0, tiled=True)


def join(parts):
    return jnp.concatenate(parts, axis=0)


def stack_rows(parts, rows):
    total, start = None, 0
    for part in parts:
        here = lax.pad(part, jnp.zeros((), BF), ((start, rows - start - part.shape[0], 0), (0, 0, 0)))
        total = here if total is None else total + here
        start += part.shape[0]
    return total


def finish(part, data):
    rows = part.shape[0] // 2
    own = jnp.where(data == 0, part[:rows], part[rows:])
    other = swap(jnp.where(data == 0, part[rows:], part[:rows]), ("dp",))
    return jnp.where(
        data == 0, jnp.concatenate([own, other], axis=1), jnp.concatenate([other, own], axis=1)
    ).astype(BF)


def dot(left, right, dims):
    return lax.dot_general(left, right, (dims, ((), ())), preferred_element_type=F32)


def per_device(
    tokens, routes, route_gates, cotangent, dense_gate, dense_up, dense_down,
    expert_gate, expert_up, expert_down,
):
    width = expert_gate.shape[2]
    hidden = expert_gate.shape[1]
    data, near, core = (lax.axis_index(name) for name in ("dp", "xlo", "core"))
    rows = tokens.shape[0]
    depth = lax.axis_size("z")

    def columns(array, at):
        return lax.dynamic_slice_in_dim(array, at * width, width, axis=1)

    ids = jnp.arange(128, dtype=jnp.int32)
    weights_of = jnp.sum(
        jnp.where(routes[:, :, None] == ids[None, None, :], route_gates.astype(F32)[:, :, None], 0.0), axis=1
    ).astype(BF)
    blank = jnp.zeros_like(weights_of)
    tok_own = jnp.concatenate([columns(tokens, data), weights_of], axis=1)
    tok_far = jnp.concatenate([columns(tokens, 1 - data), weights_of], axis=1)
    cot_own = jnp.concatenate([columns(cotangent, data), blank], axis=1)
    cot_far = jnp.concatenate([columns(cotangent, 1 - data), blank], axis=1)
    by_dp = swap(join([tok_far, cot_far]), ("dp",))
    block = join([in_order(data, tok_own, by_dp[:rows]), in_order(data, cot_own, by_dp[rows:])])
    block = gather(block, "z").reshape(depth, 2, 2 * rows, -1)

    gate_up = jnp.concatenate([expert_gate, expert_up], axis=0)
    gate_up_x = swap(gate_up, ("xlo",))
    gate_up_c = swap(gate_up, ("core",))
    down = expert_down[0]
    down_c = swap(down, ("core",))
    down_x = swap(lax.optimization_barrier((down, gate_up_x))[0], ("xlo",))
    gate_up_b = swap(gate_up_x, ("core",))
    down_b = swap(down_x, ("core",))

    units = -(-5 * hidden // 128) * 128
    expert_units = 4 * hidden

    def pack(mine, by_core, by_x, by_both, dense):
        return stack_rows([mine, by_core, by_x, by_both, columns(dense, data)], units)

    gate, up = (
        pack(gate_up[at], gate_up_c[at], gate_up_x[at], gate_up_b[at], dense)
        for at, dense in ((0, dense_gate), (1, dense_up))
    )
    down = pack(down, down_c, down_x, down_b, dense_down)

    tok = gather(block[:, 0].reshape(-1, block.shape[3]), "y").reshape(-1, block.shape[3])
    cot = gather(block[:, 1, :, :width].reshape(-1, width), "y").reshape(-1, width)

    weighting = tok[:, width:].astype(F32)
    tok = tok[:, :width]
    expert_id = near * lax.axis_size("core") + core
    unit = jnp.arange(units, dtype=jnp.int32)[None]
    scale = jnp.ones((), F32)
    for at, other in enumerate((core, 1 - core, core, 1 - core)):
        place = (near if at < 2 else 1 - near) * 2 + other
        column = jnp.sum(jnp.where(ids[None] == place, weighting, 0.0), axis=1, keepdims=True)
        scale = jnp.where((unit >= at * hidden) & (unit < (at + 1) * hidden), column, scale)

    def over_width(left, right):
        part = dot(left, right, ((1,), (1,))).astype(BF)
        return part.astype(F32) + swap(part, ("dp",)).astype(F32)

    pre, lin = over_width(tok, gate), over_width(tok, up)
    sig = jax.nn.sigmoid(pre)
    act = (pre * sig * lin * scale).astype(BF)
    dact = over_width(cot, down) * scale
    gate_grad = (dact * lin * (sig * (1.0 + pre * (1.0 - sig)))).astype(BF)
    lin_grad = (dact * (pre * sig)).astype(BF)

    def far_grads(left, right):
        term = dot(left[:, :expert_units], right, ((0,), (0,))).astype(BF)
        mine, by_core, by_x, by_both = [term[i * hidden:(i + 1) * hidden] for i in range(4)]
        landed = swap(jnp.stack([by_core, by_both]), ("core",)).astype(F32)
        return mine.astype(F32) + landed[0], (by_x.astype(F32) + landed[1]).astype(BF)

    def whole_grad(near_part, far_part):
        return (near_part + swap(far_part, ("xlo",)).astype(F32)).astype(BF)[None]

    mixed = scatter(dot(act, down, ((1,), (0,))).astype(BF), "y").astype(BF)
    grads = (dot(gate_grad, gate, ((1,), (0,))) + dot(lin_grad, up, ((1,), (0,)))).astype(BF)
    down_near, down_far = far_grads(act, cot)
    grads, down_far = lax.optimization_barrier((grads, down_far))
    grad_down = whole_grad(down_near, down_far)
    grads = scatter(grads, "y").astype(BF)
    gate_near, gate_far = far_grads(gate_grad, tok)
    up_near, up_far = far_grads(lin_grad, tok)
    both = jnp.concatenate([mixed.reshape(depth, -1, width), grads.reshape(depth, -1, width)], axis=1)
    both, gate_far, up_far, grad_down = lax.optimization_barrier((both, gate_far, up_far, grad_down))
    grad_gate, grad_up = whole_grad(gate_near, gate_far), whole_grad(up_near, up_far)
    both = scatter(both.reshape(-1, width), "z")
    mixed, grads = finish(both[:2 * rows], data), finish(both[2 * rows:], data)
    return (mixed, grads, grad_gate, grad_up, grad_down)


def solution(mesh):
    fine = Mesh(mesh.devices.reshape(2, 2, 2, 8, 4), ("dp", "xlo", "core", "z", "y"))
    every = ("dp", "xlo", "core", "z", "y")
    row = P(every, None)
    dense = P(("z", "y"), None)
    expert = P(("xlo", "core"), ("z", "y"), "dp")
    return jax.shard_map(
        per_device,
        mesh=fine,
        in_specs=(row, row, row, row, dense, dense, dense, expert, expert, expert),
        out_specs=(row, row, expert, expert, expert),
        check_vma=False,
    )
```

```python
import jax
import jax.numpy as jnp
from jax import lax
from jax.sharding import Mesh, PartitionSpec as P

BF = jnp.bfloat16
F32 = jnp.float32


def swap(value, axes):
    size = 1
    for axis in axes:
        size *= lax.axis_size(axis)
    return lax.ppermute(value, axes, [(i, size - 1 - i) for i in range(size)])


def scatter(part, axis):
    size = lax.axis_size(axis)
    landed = lax.all_to_all(part.reshape(size, -1, part.shape[1]), axis, 0, 0, tiled=True)
    return jnp.sum(landed.astype(F32), axis=0)


def gather(block, axis):
    size = lax.axis_size(axis)
    wide = jnp.broadcast_to(block[None], (size,) + block.shape)
    return lax.all_to_all(wide, axis, 0, 0, tiled=True)


def join(parts):
    return jnp.concatenate(parts, axis=0)


def stack_rows(parts, rows):
    total, start = None, 0
    for part in parts:
        here = lax.pad(part, jnp.zeros((), BF), ((start, rows - start - part.shape[0], 0), (0, 0, 0)))
        total = here if total is None else total + here
        start += part.shape[0]
    return total


def dot(left, right, dims):
    return lax.dot_general(left, right, (dims, ((), ())), preferred_element_type=F32)


def per_device(
    tokens, routes, route_gates, cotangent, dense_gate, dense_up, dense_down,
    expert_gate, expert_up, expert_down,
):
    width = expert_gate.shape[2]
    hidden = expert_gate.shape[1]
    data, near, core = (lax.axis_index(name) for name in ("dp", "xlo", "core"))
    rows = tokens.shape[0]
    halves, depth = lax.axis_size("dp"), lax.axis_size("z")

    gate_up = jnp.concatenate([expert_gate, expert_up], axis=0)
    gate_up_x = swap(gate_up, ("xlo",))
    gate_up_c = swap(gate_up, ("core",))
    down_x = swap(expert_down[0], ("xlo",))
    down_c = swap(expert_down[0], ("core",))

    def pack(mine, by_core, dense):
        dense = lax.dynamic_slice_in_dim(dense, data * width, width, axis=1)
        return stack_rows([mine, by_core, dense], 3 * hidden)

    gate_a = pack(expert_gate[0], gate_up_c[0], dense_gate)
    up_a = pack(expert_up[0], gate_up_c[1], dense_up)
    down_a = pack(expert_down[0], down_c, dense_down)

    ids = jnp.arange(128, dtype=jnp.int32)
    weights_of = jnp.sum(
        jnp.where(routes[:, :, None] == ids[None, None, :], route_gates.astype(F32)[:, :, None], 0.0), axis=1
    ).astype(BF)
    both = join([tokens, cotangent])
    marks = join([weights_of, jnp.zeros_like(weights_of)])
    both = jnp.stack([jnp.concatenate([both[:, i * width:(i + 1) * width], marks], axis=1) for i in range(halves)])
    wide = jnp.broadcast_to(both[:, None], (halves, depth) + both.shape[1:]).reshape((-1,) + both.shape[1:])
    block = lax.all_to_all(wide, ("dp", "z"), 0, 0, tiled=True)
    block, gate_a, up_a, down_a = lax.optimization_barrier((block, gate_a, up_a, down_a))

    tok = gather(block[:, :rows].reshape(-1, block.shape[2]), "y").reshape(-1, block.shape[2])
    tok, block, gate_up_x, down_x = lax.optimization_barrier((tok, block, gate_up_x, down_x))
    cot = gather(block[:, rows:, :width].reshape(-1, width), "y").reshape(-1, width)

    gate_up_b = swap(gate_up_x, ("core",))
    gate_b = stack_rows([gate_up_x[0], gate_up_b[0]], 2 * hidden)
    up_b = stack_rows([gate_up_x[1], gate_up_b[1]], 2 * hidden)
    down_b = stack_rows([down_x, swap(down_x, ("core",))], 2 * hidden)

    weighting = tok[:, width:].astype(F32)
    tok = tok[:, :width]

    def weight_column(chip, other):
        place = chip * lax.axis_size("core") + other
        return jnp.sum(jnp.where(ids[None] == place, weighting, 0.0), axis=1, keepdims=True)

    unit = jnp.arange(3 * hidden, dtype=jnp.int32)[None]
    scale_a = jnp.where(
        unit < hidden, weight_column(near, core), jnp.where(unit < 2 * hidden, weight_column(near, 1 - core), 1.0)
    )
    scale_b = jnp.where(
        unit[:, :2 * hidden] < hidden, weight_column(1 - near, core), weight_column(1 - near, 1 - core)
    )

    def over_width(left, right):
        part = dot(left, right, ((1,), (1,))).astype(BF)
        return part.astype(F32) + swap(part, ("dp",)).astype(F32)

    def forward(gate, up, scale):
        pre, lin = over_width(tok, gate), over_width(tok, up)
        return pre, lin, (jax.nn.silu(pre) * lin * scale).astype(BF)

    def backward(pre, lin, down, scale):
        dact = over_width(cot, down) * scale
        sig = jax.nn.sigmoid(pre)
        return (dact * lin * (sig * (1.0 + pre * (1.0 - sig)))).astype(BF), (dact * (pre * sig)).astype(BF)

    pre_a, lin_a, act_a = forward(gate_a, up_a, scale_a)
    pre_b, lin_b, act_b = forward(gate_b, up_b, scale_b)
    grad_a, lin_grad_a = backward(pre_a, lin_a, down_a, scale_a)
    grad_b, lin_grad_b = backward(pre_b, lin_b, down_b, scale_b)

    def times(*pairs):
        return sum(dot(left, right, ((1,), (0,))) for left, right in pairs).astype(BF)

    mixed = scatter(times((act_a, down_a), (act_b, down_b)), "y").astype(BF)
    grads = times((grad_a, gate_a), (lin_grad_a, up_a), (grad_b, gate_b), (lin_grad_b, up_b))

    def far_grads(left_a, left_b, right):
        ours = jnp.concatenate([left_a[:, :hidden], left_b[:, :hidden]], axis=1)
        theirs = jnp.concatenate([left_a[:, hidden:2 * hidden], left_b[:, hidden:]], axis=1)
        ours, theirs = [dot(left, right, ((0,), (0,))).astype(BF) for left in (ours, theirs)]
        theirs = swap(theirs, ("core",))
        return ours, theirs, (ours[hidden:].astype(F32) + theirs[hidden:].astype(F32)).astype(BF)

    def whole_grad(ours, theirs, far):
        far = swap(far, ("xlo",))
        return (ours[:hidden].astype(F32) + theirs[:hidden].astype(F32) + far.astype(F32)).astype(BF)[None]

    parts = [far_grads(act_a, act_b, cot), far_grads(grad_a, grad_b, tok), far_grads(lin_grad_a, lin_grad_b, tok)]
    grads, parts = lax.optimization_barrier((grads, parts))
    grad_down, grad_gate, grad_up = [whole_grad(*part) for part in parts]
    grads = scatter(grads, "y").astype(BF)
    both = jnp.concatenate([part.reshape(halves * depth, rows, width) for part in (mixed, grads)], axis=1)
    both = lax.all_to_all(both, ("dp", "z"), 0, 0, tiled=True).astype(F32)
    both = jnp.sum(both.reshape(halves, depth, 2 * rows, width), axis=1).astype(BF)
    both = jnp.concatenate([both[i] for i in range(halves)], axis=1)
    return (both[:rows], both[rows:], grad_gate, grad_up, grad_down)


def solution(mesh):
    fine = Mesh(mesh.devices.reshape(2, 2, 2, 8, 4), ("dp", "xlo", "core", "z", "y"))
    every = ("dp", "xlo", "core", "z", "y")
    row = P(every, None)
    dense = P(("z", "y"), None)
    expert = P(("xlo", "core"), ("z", "y"), "dp")
    return jax.shard_map(
        per_device,
        mesh=fine,
        in_specs=(row, row, row, row, dense, dense, dense, expert, expert, expert),
        out_specs=(row, row, expert, expert, expert),
        check_vma=False,
    )
```

```python
import jax
import jax.numpy as jnp
from jax import lax
from jax.sharding import Mesh, PartitionSpec as P

BF = jnp.bfloat16
F32 = jnp.float32


def swap(value, axes):
    size = 1
    for axis in axes:
        size *= lax.axis_size(axis)
    return lax.ppermute(value, axes, [(i, size - 1 - i) for i in range(size)])


def scatter(part, axis):
    size = lax.axis_size(axis)
    landed = lax.all_to_all(part.reshape(size, -1, part.shape[1]), axis, 0, 0, tiled=True)
    return jnp.sum(landed.astype(F32), axis=0)


def in_order(data, mine, other):
    return jnp.where(data == 0, jnp.concatenate([mine, other], axis=0), jnp.concatenate([other, mine], axis=0))


def gather(block, axis):
    size = lax.axis_size(axis)
    wide = jnp.broadcast_to(block[None], (size,) + block.shape)
    return lax.all_to_all(wide, axis, 0, 0, tiled=True)


def join(parts):
    return jnp.concatenate(parts, axis=0)


def stack_rows(parts, rows):
    total, start = None, 0
    for part in parts:
        here = lax.pad(part, jnp.zeros((), BF), ((start, rows - start - part.shape[0], 0), (0, 0, 0)))
        total = here if total is None else total + here
        start += part.shape[0]
    return total


def finish(part, data):
    rows = part.shape[0] // 2
    own = jnp.where(data == 0, part[:rows], part[rows:])
    other = swap(jnp.where(data == 0, part[rows:], part[:rows]), ("dp",))
    return jnp.where(
        data == 0, jnp.concatenate([own, other], axis=1), jnp.concatenate([other, own], axis=1)
    ).astype(BF)


def dot(left, right, dims):
    return lax.dot_general(left, right, (dims, ((), ())), preferred_element_type=F32)


def per_device(
    tokens, routes, route_gates, cotangent, dense_gate, dense_up, dense_down,
    expert_gate, expert_up, expert_down,
):
    width = expert_gate.shape[2]
    hidden = expert_gate.shape[1]
    data, near, core = (lax.axis_index(name) for name in ("dp", "xlo", "core"))
    rows = tokens.shape[0]
    depth = lax.axis_size("z")

    gate, up, down = expert_gate[0], expert_up[0], expert_down[0]
    gate_x = swap(gate, ("xlo",))

    def pack(mine, dense):
        dense = lax.dynamic_slice_in_dim(dense, data * width, width, axis=1)
        return stack_rows([mine, swap(mine, ("core",)), dense], 3 * hidden)

    def pack_far(theirs):
        return stack_rows([theirs, swap(theirs, ("core",))], 2 * hidden)

    gate_a, up_a, down_a = pack(gate, dense_gate), pack(up, dense_up), pack(down, dense_down)

    ids = jnp.arange(128, dtype=jnp.int32)
    weights_of = jnp.sum(
        jnp.where(routes[:, :, None] == ids[None, None, :], route_gates.astype(F32)[:, :, None], 0.0), axis=1
    ).astype(BF)
    marks = join([weights_of, jnp.zeros_like(weights_of)])

    def columns(at):
        both = lax.dynamic_slice_in_dim(join([tokens, cotangent]), at * width, width, axis=1)
        return jnp.concatenate([both, marks], axis=1)

    own, far = columns(data), swap(columns(1 - data), ("dp",))
    block = join([in_order(data, own[:rows], far[:rows]), in_order(data, own[rows:], far[rows:])])
    block = gather(block, "z").reshape(depth, 4 * rows, -1)
    block, gate_x, gate_a, up_a, down_a, up = lax.optimization_barrier((block, gate_x, gate_a, up_a, down_a, up))
    up_x = swap(up, ("xlo",))
    tok = gather(block[:, :2 * rows].reshape(-1, block.shape[2]), "y").reshape(-1, block.shape[2])
    gate_b = pack_far(gate_x)
    block, tok, up_x, down = lax.optimization_barrier((block, tok, up_x, down))
    down_x = swap(down, ("xlo",))
    cot = gather(block[:, 2 * rows:, :width].reshape(-1, width), "y").reshape(-1, width)
    up_b = pack_far(up_x)

    weighting = tok[:, width:].astype(F32)
    tok = tok[:, :width]

    def weight_column(chip, other):
        place = chip * lax.axis_size("core") + other
        return jnp.sum(jnp.where(ids[None] == place, weighting, 0.0), axis=1, keepdims=True)

    unit = jnp.arange(3 * hidden, dtype=jnp.int32)[None]
    scale_a = jnp.where(
        unit < hidden, weight_column(near, core), jnp.where(unit < 2 * hidden, weight_column(near, 1 - core), 1.0)
    )
    scale_b = jnp.where(
        unit[:, :2 * hidden] < hidden, weight_column(1 - near, core), weight_column(1 - near, 1 - core)
    )

    def over_width(left, right):
        part = dot(left, right, ((1,), (1,))).astype(BF)
        return part.astype(F32) + swap(part, ("dp",)).astype(F32)

    def forward(gate, up, scale):
        pre, lin = over_width(tok, gate), over_width(tok, up)
        return pre, lin, (jax.nn.silu(pre) * lin * scale).astype(BF)

    def backward(pre, lin, down, scale):
        dact = over_width(cot, down) * scale
        sig = jax.nn.sigmoid(pre)
        return (dact * lin * (sig * (1.0 + pre * (1.0 - sig)))).astype(BF), (dact * (pre * sig)).astype(BF)

    pre_a, lin_a, act_a = forward(gate_a, up_a, scale_a)
    pre_b, lin_b, act_b = forward(gate_b, up_b, scale_b)
    cot, down_x, act_a, act_b = lax.optimization_barrier((cot, down_x, act_a, act_b))
    down_b = pack_far(down_x)
    grad_a, lin_grad_a = backward(pre_a, lin_a, down_a, scale_a)
    grad_b, lin_grad_b = backward(pre_b, lin_b, down_b, scale_b)

    def times(*pairs):
        return sum(dot(left, right, ((1,), (0,))) for left, right in pairs).astype(BF)

    mixed = times((act_a, down_a), (act_b, down_b))
    grads = times((grad_a, gate_a), (lin_grad_a, up_a), (grad_b, gate_b), (lin_grad_b, up_b))

    def far_grads(left_a, left_b, right):
        ours = jnp.concatenate([left_a[:, :hidden], left_b[:, :hidden]], axis=1)
        theirs = jnp.concatenate([left_a[:, hidden:2 * hidden], left_b[:, hidden:]], axis=1)
        ours, theirs = [dot(left, right, ((0,), (0,))).astype(BF) for left in (ours, theirs)]
        theirs = swap(theirs, ("core",))
        return ours, theirs, (ours[hidden:].astype(F32) + theirs[hidden:].astype(F32)).astype(BF)

    def whole_grad(ours, theirs, far):
        return (ours[:hidden].astype(F32) + theirs[:hidden].astype(F32) + far.astype(F32)).astype(BF)[None]

    down_ours, down_theirs, down_far = far_grads(act_a, act_b, cot)
    mixed, down_far = lax.optimization_barrier((mixed, down_far))
    down_far = swap(down_far, ("xlo",))
    mixed = scatter(mixed, "y").astype(BF)
    gate_ours, gate_theirs, gate_far = far_grads(grad_a, grad_b, tok)
    grads, gate_far, mixed, down_far = lax.optimization_barrier((grads, gate_far, mixed, down_far))
    gate_far = swap(gate_far, ("xlo",))
    grads = scatter(grads, "y").astype(BF)
    up_ours, up_theirs, up_far = far_grads(lin_grad_a, lin_grad_b, tok)
    both = jnp.concatenate([part.reshape(depth, 2 * rows, width) for part in (mixed, grads)], axis=1)
    both, up_far, gate_far = lax.optimization_barrier((both, up_far, gate_far))
    up_far = swap(up_far, ("xlo",))
    both = scatter(both.reshape(-1, width), "z")
    mixed, grads = finish(both[:2 * rows], data), finish(both[2 * rows:], data)
    return (
        mixed,
        grads,
        whole_grad(gate_ours, gate_theirs, gate_far),
        whole_grad(up_ours, up_theirs, up_far),
        whole_grad(down_ours, down_theirs, down_far),
    )


def solution(mesh):
    fine = Mesh(mesh.devices.reshape(2, 2, 2, 8, 4), ("dp", "xlo", "core", "z", "y"))
    every = ("dp", "xlo", "core", "z", "y")
    row = P(every, None)
    dense = P(("z", "y"), None)
    expert = P(("xlo", "core"), ("z", "y"), "dp")
    return jax.shard_map(
        per_device,
        mesh=fine,
        in_specs=(row, row, row, row, dense, dense, dense, expert, expert, expert),
        out_specs=(row, row, expert, expert, expert),
        check_vma=False,
    )
```

```python
import jax
import jax.numpy as jnp
from jax import lax
from jax.sharding import Mesh, PartitionSpec as P

BF = jnp.bfloat16
F32 = jnp.float32


def swap(value, axes):
    size = 1
    for axis in axes:
        size *= lax.axis_size(axis)
    return lax.ppermute(value, axes, [(i, size - 1 - i) for i in range(size)])


def scatter(part, axis):
    size = lax.axis_size(axis)
    landed = lax.all_to_all(part.reshape(size, -1, part.shape[1]), axis, 0, 0, tiled=True)
    return jnp.sum(landed.astype(F32), axis=0)


def in_order(data, mine, other):
    return jnp.where(data == 0, jnp.concatenate([mine, other], axis=0), jnp.concatenate([other, mine], axis=0))


def gather(block, axis):
    size = lax.axis_size(axis)
    wide = jnp.broadcast_to(block[None], (size,) + block.shape)
    return lax.all_to_all(wide, axis, 0, 0, tiled=True)


def join(parts):
    return jnp.concatenate(parts, axis=0)


def place(buffer, part, at):
    return lax.dynamic_update_slice_in_dim(buffer, part, at, axis=0)


def finish(part, data):
    rows = part.shape[0] // 2
    own = jnp.where(data == 0, part[:rows], part[rows:])
    other = swap(jnp.where(data == 0, part[rows:], part[:rows]), ("dp",))
    return jnp.where(
        data == 0, jnp.concatenate([own, other], axis=1), jnp.concatenate([other, own], axis=1)
    ).astype(BF)


def dot(left, right, dims):
    return lax.dot_general(left, right, (dims, ((), ())), preferred_element_type=F32)


def per_device(
    tokens, routes, route_gates, cotangent, dense_gate, dense_up, dense_down,
    expert_gate, expert_up, expert_down,
):
    width = expert_gate.shape[2]
    hidden = expert_gate.shape[1]
    data, near, core = (lax.axis_index(name) for name in ("dp", "xlo", "core"))
    rows = tokens.shape[0]
    depth = lax.axis_size("z")

    ids = jnp.arange(128, dtype=jnp.int32)
    weights_of = jnp.sum(
        jnp.where(routes[:, :, None] == ids[None, None, :], route_gates.astype(F32)[:, :, None], 0.0), axis=1
    ).astype(BF)
    marks = join([weights_of, jnp.zeros_like(weights_of)])

    def columns(at):
        both = lax.dynamic_slice_in_dim(join([tokens, cotangent]), at * width, width, axis=1)
        return jnp.concatenate([both, marks], axis=1)

    own, far = columns(data), swap(columns(1 - data), ("dp",))
    block = join([in_order(data, own[:rows], far[:rows]), in_order(data, own[rows:], far[rows:])])
    block = gather(block, "z").reshape(depth, 4 * rows, -1)

    gate, up, down = expert_gate[0], expert_up[0], expert_down[0]
    units = -(-5 * hidden // 128) * 128
    _, gate = lax.optimization_barrier((far, gate))
    gate_x = swap(gate, ("xlo",))

    def columns_of(dense):
        return lax.dynamic_slice_in_dim(dense, data * width, width, axis=1)

    def place_near(buffer, mine, dense, at):
        buffer = place(buffer, mine, at)
        buffer = place(buffer, swap(mine, ("core",)), at + 2 * hidden)
        return place(buffer, columns_of(dense), at + 4 * hidden)

    def place_far(buffer, theirs, at):
        buffer = place(buffer, theirs, at + hidden)
        return place(buffer, swap(theirs, ("core",)), at + 3 * hidden)

    pair = jnp.zeros((2 * units, width), BF)
    pair = place_near(place_near(pair, gate, dense_gate, 0), up, dense_up, units)
    last = place_near(jnp.zeros((units, width), BF), down, dense_down, 0)

    block, gate_x, pair, last, up = lax.optimization_barrier((block, gate_x, pair, last, up))
    up_x = swap(up, ("xlo",))
    tok = gather(block[:, :2 * rows].reshape(-1, block.shape[2]), "y").reshape(-1, block.shape[2])
    pair = place_far(pair, gate_x, 0)
    block, tok, up_x, down, pair = lax.optimization_barrier((block, tok, up_x, down, pair))
    down_x = swap(down, ("xlo",))
    cot = gather(block[:, 2 * rows:, :width].reshape(-1, width), "y").reshape(-1, width)
    pair = place_far(pair, up_x, units)

    weighting = tok[:, width:].astype(F32)
    tok = tok[:, :width]

    unit = jnp.arange(units, dtype=jnp.int32)[None]
    scale = jnp.ones((), F32)
    for at, chip, other in ((0, near, core), (1, 1 - near, core), (2, near, 1 - core), (3, 1 - near, 1 - core)):
        column = jnp.sum(
            jnp.where(ids[None] == chip * lax.axis_size("core") + other, weighting, 0.0), axis=1, keepdims=True
        )
        scale = jnp.where((unit >= at * hidden) & (unit < (at + 1) * hidden), column, scale)

    both = dot(tok, pair, ((1,), (1,))).astype(BF)
    both, down_x, cot = lax.optimization_barrier((both, down_x, cot))
    last = place_far(last, down_x, 0)
    dact = dot(cot, last, ((1,), (1,))).astype(BF)
    far_both, _ = lax.optimization_barrier((swap(both, ("dp",)), dact))
    both = both.astype(F32) + far_both.astype(F32)
    dact = dact.astype(F32) + swap(dact, ("dp",)).astype(F32)
    pre, lin = both[:, :units], both[:, units:]
    sig = jax.nn.sigmoid(pre)
    act = (pre * sig * lin * scale).astype(BF)
    gate_slope = lin * scale * (sig * (1.0 + pre * (1.0 - sig)))
    lin_slope = pre * sig * scale
    mixed = dot(act, last, ((1,), (0,))).astype(BF)

    def far_grads(left, right):
        ours = dot(left[:, :2 * hidden], right, ((0,), (0,))).astype(BF)
        theirs = swap(dot(left[:, 2 * hidden:4 * hidden], right, ((0,), (0,))).astype(BF), ("core",))
        return ours, theirs, (ours[hidden:].astype(F32) + theirs[hidden:].astype(F32)).astype(BF)

    def whole_grad(ours, theirs, far):
        return (ours[:hidden].astype(F32) + theirs[:hidden].astype(F32) + far.astype(F32)).astype(BF)[None]

    down_ours, down_theirs, down_far = far_grads(act, cot)
    mixed, down_far = lax.optimization_barrier((mixed, down_far))
    dact, _ = lax.optimization_barrier((dact, mixed))
    down_far = swap(down_far, ("xlo",))
    mixed = scatter(mixed, "y").astype(BF)
    slopes = jnp.concatenate([dact * gate_slope, dact * lin_slope], axis=1).astype(BF)
    grads = dot(slopes, pair, ((1,), (0,))).astype(BF)
    gate_ours, gate_theirs, gate_far = far_grads(slopes[:, :units], tok)
    grads, gate_far, mixed, down_far = lax.optimization_barrier((grads, gate_far, mixed, down_far))
    gate_far = swap(gate_far, ("xlo",))
    grads = scatter(grads, "y").astype(BF)
    up_ours, up_theirs, up_far = far_grads(slopes[:, units:], tok)
    both = jnp.concatenate([part.reshape(depth, 2 * rows, width) for part in (mixed, grads)], axis=1)
    both, up_far, gate_far = lax.optimization_barrier((both, up_far, gate_far))
    up_far = swap(up_far, ("xlo",))
    both = scatter(both.reshape(-1, width), "z")
    mixed, grads = finish(both[:2 * rows], data), finish(both[2 * rows:], data)
    return (
        mixed,
        grads,
        whole_grad(gate_ours, gate_theirs, gate_far),
        whole_grad(up_ours, up_theirs, up_far),
        whole_grad(down_ours, down_theirs, down_far),
    )


def solution(mesh):
    fine = Mesh(mesh.devices.reshape(2, 2, 2, 8, 4), ("dp", "xlo", "core", "z", "y"))
    every = ("dp", "xlo", "core", "z", "y")
    row = P(every, None)
    dense = P(("z", "y"), None)
    expert = P(("xlo", "core"), ("z", "y"), "dp")
    return jax.shard_map(
        per_device,
        mesh=fine,
        in_specs=(row, row, row, row, dense, dense, dense, expert, expert, expert),
        out_specs=(row, row, expert, expert, expert),
        check_vma=False,
    )
```

```python
import jax
import jax.numpy as jnp
from jax import lax
from jax.sharding import Mesh, PartitionSpec as P

BF = jnp.bfloat16
F32 = jnp.float32


def swap(value, axes):
    size = 1
    for axis in axes:
        size *= lax.axis_size(axis)
    return lax.ppermute(value, axes, [(i, size - 1 - i) for i in range(size)])


def scatter(part, axis):
    size = lax.axis_size(axis)
    landed = lax.all_to_all(part.reshape(size, -1, part.shape[1]), axis, 0, 0, tiled=True)
    return jnp.sum(landed.astype(F32), axis=0)


def in_order(data, mine, other):
    return jnp.where(data == 0, jnp.concatenate([mine, other], axis=0), jnp.concatenate([other, mine], axis=0))


def gather(block, axis):
    size = lax.axis_size(axis)
    wide = jnp.broadcast_to(block[None], (size,) + block.shape)
    return lax.all_to_all(wide, axis, 0, 0, tiled=True)


def join(parts):
    return jnp.concatenate(parts, axis=0)


def place(buffer, part, at):
    return lax.dynamic_update_slice_in_dim(buffer, part, at, axis=0)


def finish(part, data):
    rows = part.shape[0] // 2
    own = jnp.where(data == 0, part[:rows], part[rows:])
    other = swap(jnp.where(data == 0, part[rows:], part[:rows]), ("dp",))
    return jnp.where(
        data == 0, jnp.concatenate([own, other], axis=1), jnp.concatenate([other, own], axis=1)
    ).astype(BF)


def dot(left, right, dims):
    return lax.dot_general(left, right, (dims, ((), ())), preferred_element_type=F32)


def per_device(
    tokens, routes, route_gates, cotangent, dense_gate, dense_up, dense_down,
    expert_gate, expert_up, expert_down,
):
    width = expert_gate.shape[2]
    hidden = expert_gate.shape[1]
    data, near, core = (lax.axis_index(name) for name in ("dp", "xlo", "core"))
    rows = tokens.shape[0]
    depth = lax.axis_size("z")

    ids = jnp.arange(128, dtype=jnp.int32)
    weights_of = jnp.sum(
        jnp.where(routes[:, :, None] == ids[None, None, :], route_gates.astype(F32)[:, :, None], 0.0), axis=1
    ).astype(BF)
    marks = join([weights_of, jnp.zeros_like(weights_of)])

    def columns(at):
        both = lax.dynamic_slice_in_dim(join([tokens, cotangent]), at * width, width, axis=1)
        return jnp.concatenate([both, marks], axis=1)

    own, far = columns(data), swap(columns(1 - data), ("dp",))
    tok = in_order(data, own[:rows], far[:rows])
    cot = in_order(data, own[rows:, :width], far[rows:, :width])
    tok = gather(tok, "z").reshape(-1, tok.shape[1])

    gate, up, down = expert_gate[0], expert_up[0], expert_down[0]
    units = -(-5 * hidden // 128) * 128
    _, gate_late = lax.optimization_barrier((far, gate))
    gate_x = swap(gate_late, ("xlo",))

    def columns_of(dense):
        return lax.dynamic_slice_in_dim(dense, data * width, width, axis=1)

    def place_near(buffer, mine, dense, at):
        buffer = place(buffer, mine, at)
        buffer = place(buffer, swap(mine, ("core",)), at + 2 * hidden)
        return place(buffer, columns_of(dense), at + 4 * hidden)

    def place_far(buffer, theirs, at):
        buffer = place(buffer, theirs, at + hidden)
        return place(buffer, swap(theirs, ("core",)), at + 3 * hidden)

    pair = jnp.zeros((2 * units, width), BF)
    pair = place_near(place_near(pair, gate, dense_gate, 0), up, dense_up, units)

    tok, gate_x, pair, up, down = lax.optimization_barrier((tok, gate_x, pair, up, down))
    up_x = swap(up, ("xlo",))
    tok = gather(tok, "y").reshape(-1, tok.shape[1])
    pair = place_far(pair, gate_x, 0)
    last = place_near(jnp.zeros((units, width), BF), down, dense_down, 0)
    cot, tok, up_x, down, pair, last = lax.optimization_barrier((cot, tok, up_x, down, pair, last))
    down_x = swap(down, ("xlo",))
    cot = gather(gather(cot, "z").reshape(-1, width), "y").reshape(-1, width)
    pair = place_far(pair, up_x, units)

    weighting = tok[:, width:].astype(F32)
    tok = tok[:, :width]

    unit = jnp.arange(units, dtype=jnp.int32)[None]
    scale = jnp.ones((), F32)
    for at, chip, other in ((0, near, core), (1, 1 - near, core), (2, near, 1 - core), (3, 1 - near, 1 - core)):
        column = jnp.sum(
            jnp.where(ids[None] == chip * lax.axis_size("core") + other, weighting, 0.0), axis=1, keepdims=True
        )
        scale = jnp.where((unit >= at * hidden) & (unit < (at + 1) * hidden), column, scale)

    both = dot(tok, pair, ((1,), (1,))).astype(BF)
    both, down_x = lax.optimization_barrier((both, down_x))
    last = place_far(last, down_x, 0)
    dact = dot(cot, last, ((1,), (1,))).astype(BF)
    both = both.astype(F32) + swap(both, ("dp",)).astype(F32)
    pre, lin = both[:, :units], both[:, units:]
    sig = jax.nn.sigmoid(pre)
    act = (pre * sig * lin * scale).astype(BF)
    gate_slope = lin * scale * (sig * (1.0 + pre * (1.0 - sig)))
    lin_slope = pre * sig * scale
    mixed = dot(act, last, ((1,), (0,))).astype(BF)

    def far_grads(left, right):
        ours = dot(left[:, :2 * hidden], right, ((0,), (0,))).astype(BF)
        theirs = swap(dot(left[:, 2 * hidden:4 * hidden], right, ((0,), (0,))).astype(BF), ("core",))
        return ours, theirs, (ours[hidden:].astype(F32) + theirs[hidden:].astype(F32)).astype(BF)

    def whole_grad(ours, theirs, far):
        return (ours[:hidden].astype(F32) + theirs[:hidden].astype(F32) + far.astype(F32)).astype(BF)[None]

    down_ours, down_theirs, down_far = far_grads(act, cot)
    mixed, down_far = lax.optimization_barrier((mixed, down_far))
    far_dact, _ = lax.optimization_barrier((swap(dact, ("dp",)), mixed))
    dact = dact.astype(F32) + far_dact.astype(F32)
    down_far = swap(down_far, ("xlo",))
    mixed = scatter(mixed, "y").astype(BF)
    slopes = jnp.concatenate([dact * gate_slope, dact * lin_slope], axis=1).astype(BF)
    grads = dot(slopes, pair, ((1,), (0,))).astype(BF)
    gate_ours, gate_theirs, gate_far = far_grads(slopes[:, :units], tok)
    grads, gate_far, mixed, down_far = lax.optimization_barrier((grads, gate_far, mixed, down_far))
    gate_far = swap(gate_far, ("xlo",))
    grads = scatter(grads, "y").astype(BF)
    up_ours, up_theirs, up_far = far_grads(slopes[:, units:], tok)
    both = jnp.concatenate([part.reshape(depth, 2 * rows, width) for part in (mixed, grads)], axis=1)
    both, up_far, gate_far = lax.optimization_barrier((both, up_far, gate_far))
    up_far = swap(up_far, ("xlo",))
    both = scatter(both.reshape(-1, width), "z")
    mixed, grads = finish(both[:2 * rows], data), finish(both[2 * rows:], data)
    return (
        mixed,
        grads,
        whole_grad(gate_ours, gate_theirs, gate_far),
        whole_grad(up_ours, up_theirs, up_far),
        whole_grad(down_ours, down_theirs, down_far),
    )


def solution(mesh):
    fine = Mesh(mesh.devices.reshape(2, 2, 2, 8, 4), ("dp", "xlo", "core", "z", "y"))
    every = ("dp", "xlo", "core", "z", "y")
    row = P(every, None)
    dense = P(("z", "y"), None)
    expert = P(("xlo", "core"), ("z", "y"), "dp")
    return jax.shard_map(
        per_device,
        mesh=fine,
        in_specs=(row, row, row, row, dense, dense, dense, expert, expert, expert),
        out_specs=(row, row, expert, expert, expert),
        check_vma=False,
    )
```

```python
import jax
import jax.numpy as jnp
from jax import lax
from jax.sharding import Mesh, PartitionSpec as P

BF = jnp.bfloat16
F32 = jnp.float32


def swap(value, axes):
    size = 1
    for axis in axes:
        size *= lax.axis_size(axis)
    return lax.ppermute(value, axes, [(i, size - 1 - i) for i in range(size)])


def scatter(part, axis):
    size = lax.axis_size(axis)
    landed = lax.all_to_all(part.reshape(size, -1, part.shape[1]), axis, 0, 0, tiled=True)
    return jnp.sum(landed.astype(F32), axis=0)


def in_order(data, mine, other):
    return jnp.where(data == 0, jnp.concatenate([mine, other], axis=0), jnp.concatenate([other, mine], axis=0))


def gather(block, axis):
    size = lax.axis_size(axis)
    wide = jnp.broadcast_to(block[None], (size,) + block.shape)
    return lax.all_to_all(wide, axis, 0, 0, tiled=True)


def join(parts):
    return jnp.concatenate(parts, axis=0)


def place(buffer, part, at):
    return lax.dynamic_update_slice_in_dim(buffer, part, at, axis=0)


def finish(part, data):
    rows = part.shape[0] // 2
    own = jnp.where(data == 0, part[:rows], part[rows:])
    other = swap(jnp.where(data == 0, part[rows:], part[:rows]), ("dp",))
    return jnp.where(
        data == 0, jnp.concatenate([own, other], axis=1), jnp.concatenate([other, own], axis=1)
    ).astype(BF)


def dot(left, right, dims):
    return lax.dot_general(left, right, (dims, ((), ())), preferred_element_type=F32)


def per_device(
    tokens, routes, route_gates, cotangent, dense_gate, dense_up, dense_down,
    expert_gate, expert_up, expert_down,
):
    width = expert_gate.shape[2]
    hidden = expert_gate.shape[1]
    data, near, core = (lax.axis_index(name) for name in ("dp", "xlo", "core"))
    rows = tokens.shape[0]
    depth = lax.axis_size("z")

    ids = jnp.arange(128, dtype=jnp.int32)
    weights_of = jnp.sum(
        jnp.where(routes[:, :, None] == ids[None, None, :], route_gates.astype(F32)[:, :, None], 0.0), axis=1
    ).astype(BF)
    marks = join([weights_of, jnp.zeros_like(weights_of)])

    def columns(at):
        both = lax.dynamic_slice_in_dim(join([tokens, cotangent]), at * width, width, axis=1)
        return jnp.concatenate([both, marks], axis=1)

    own, far = columns(data), swap(columns(1 - data), ("dp",))
    block = join([in_order(data, own[:rows], far[:rows]), in_order(data, own[rows:], far[rows:])])
    block = gather(block, "z").reshape(depth, 4 * rows, -1)

    gate, up, down = expert_gate[0], expert_up[0], expert_down[0]
    units = -(-5 * hidden // 128) * 128
    _, gate = lax.optimization_barrier((far, gate))
    gate_x = swap(gate, ("xlo",))

    def columns_of(dense):
        return lax.dynamic_slice_in_dim(dense, data * width, width, axis=1)

    def place_near(buffer, mine, dense, at):
        buffer = place(buffer, mine, at)
        buffer = place(buffer, swap(mine, ("core",)), at + 2 * hidden)
        return place(buffer, columns_of(dense), at + 4 * hidden)

    def place_far(buffer, theirs, at):
        buffer = place(buffer, theirs, at + hidden)
        return place(buffer, swap(theirs, ("core",)), at + 3 * hidden)

    pair = jnp.zeros((2 * units, width), BF)
    pair = place_near(place_near(pair, gate, dense_gate, 0), up, dense_up, units)
    up_late, _ = lax.optimization_barrier((up, gate_x))
    up_x = swap(up_late, ("xlo",))
    down_late, _ = lax.optimization_barrier((down, up_x))
    down_x = swap(down_late, ("xlo",))

    block, pair, down = lax.optimization_barrier((block, pair, down))
    tok = gather(block[:, :2 * rows].reshape(-1, block.shape[2]), "y").reshape(-1, block.shape[2])
    last = place_near(jnp.zeros((units, width), BF), down, dense_down, 0)
    pair = place_far(pair, gate_x, 0)
    block, tok, pair, last = lax.optimization_barrier((block, tok, pair, last))
    cot = gather(block[:, 2 * rows:, :width].reshape(-1, width), "y").reshape(-1, width)
    pair = place_far(pair, up_x, units)

    weighting = tok[:, width:].astype(F32)
    tok = tok[:, :width]

    unit = jnp.arange(units, dtype=jnp.int32)[None]
    scale = jnp.ones((), F32)
    for at, chip, other in ((0, near, core), (1, 1 - near, core), (2, near, 1 - core), (3, 1 - near, 1 - core)):
        column = jnp.sum(
            jnp.where(ids[None] == chip * lax.axis_size("core") + other, weighting, 0.0), axis=1, keepdims=True
        )
        scale = jnp.where((unit >= at * hidden) & (unit < (at + 1) * hidden), column, scale)

    both = dot(tok, pair, ((1,), (1,))).astype(BF)
    both, down_x, cot = lax.optimization_barrier((both, down_x, cot))
    last = place_far(last, down_x, 0)
    dact = dot(cot, last, ((1,), (1,))).astype(BF)
    far_both, _ = lax.optimization_barrier((swap(both, ("dp",)), dact))
    both = both.astype(F32) + far_both.astype(F32)
    dact = dact.astype(F32) + swap(dact, ("dp",)).astype(F32)
    pre, lin = both[:, :units], both[:, units:]
    sig = jax.nn.sigmoid(pre)
    act = (pre * sig * lin * scale).astype(BF)
    gate_slope = lin * scale * (sig * (1.0 + pre * (1.0 - sig)))
    lin_slope = pre * sig * scale
    mixed = dot(act, last, ((1,), (0,))).astype(BF)

    def far_grads(left, right):
        ours = dot(left[:, :2 * hidden], right, ((0,), (0,))).astype(BF)
        theirs = swap(dot(left[:, 2 * hidden:4 * hidden], right, ((0,), (0,))).astype(BF), ("core",))
        return ours, theirs, (ours[hidden:].astype(F32) + theirs[hidden:].astype(F32)).astype(BF)

    def whole_grad(ours, theirs, far):
        return (ours[:hidden].astype(F32) + theirs[:hidden].astype(F32) + far.astype(F32)).astype(BF)[None]

    down_ours, down_theirs, down_far = far_grads(act, cot)
    mixed, down_far = lax.optimization_barrier((mixed, down_far))
    dact, _ = lax.optimization_barrier((dact, mixed))
    down_far = swap(down_far, ("xlo",))
    mixed = scatter(mixed, "y").astype(BF)
    slopes = jnp.concatenate([dact * gate_slope, dact * lin_slope], axis=1).astype(BF)
    grads = dot(slopes, pair, ((1,), (0,))).astype(BF)
    gate_ours, gate_theirs, gate_far = far_grads(slopes[:, :units], tok)
    grads, gate_far, mixed, down_far = lax.optimization_barrier((grads, gate_far, mixed, down_far))
    gate_far = swap(gate_far, ("xlo",))
    grads = scatter(grads, "y").astype(BF)
    up_ours, up_theirs, up_far = far_grads(slopes[:, units:], tok)
    both = jnp.concatenate([part.reshape(depth, 2 * rows, width) for part in (mixed, grads)], axis=1)
    both, up_far, gate_far = lax.optimization_barrier((both, up_far, gate_far))
    up_far = swap(up_far, ("xlo",))
    both = scatter(both.reshape(-1, width), "z")
    mixed, grads = finish(both[:2 * rows], data), finish(both[2 * rows:], data)
    return (
        mixed,
        grads,
        whole_grad(gate_ours, gate_theirs, gate_far),
        whole_grad(up_ours, up_theirs, up_far),
        whole_grad(down_ours, down_theirs, down_far),
    )


def solution(mesh):
    fine = Mesh(mesh.devices.reshape(2, 2, 2, 8, 4), ("dp", "xlo", "core", "z", "y"))
    every = ("dp", "xlo", "core", "z", "y")
    row = P(every, None)
    dense = P(("z", "y"), None)
    expert = P(("xlo", "core"), ("z", "y"), "dp")
    return jax.shard_map(
        per_device,
        mesh=fine,
        in_specs=(row, row, row, row, dense, dense, dense, expert, expert, expert),
        out_specs=(row, row, expert, expert, expert),
        check_vma=False,
    )
```

```python
import jax
import jax.numpy as jnp
from jax import lax
from jax.sharding import Mesh, PartitionSpec as P

BF = jnp.bfloat16
F32 = jnp.float32


def swap(value, axes):
    size = 1
    for axis in axes:
        size *= lax.axis_size(axis)
    return lax.ppermute(value, axes, [(i, size - 1 - i) for i in range(size)])


def scatter(part, axis):
    size = lax.axis_size(axis)
    landed = lax.all_to_all(part.reshape(size, -1, part.shape[1]), axis, 0, 0, tiled=True)
    return jnp.sum(landed.astype(F32), axis=0)


def in_order(data, mine, other):
    return jnp.where(data == 0, jnp.concatenate([mine, other], axis=0), jnp.concatenate([other, mine], axis=0))


def gather(block, axis):
    size = lax.axis_size(axis)
    wide = jnp.broadcast_to(block[None], (size,) + block.shape)
    return lax.all_to_all(wide, axis, 0, 0, tiled=True)


def join(parts):
    return jnp.concatenate(parts, axis=0)


def place(buffer, part, at):
    return lax.dynamic_update_slice_in_dim(buffer, part, at, axis=0)


def finish(part, data):
    rows = part.shape[0] // 2
    own = jnp.where(data == 0, part[:rows], part[rows:])
    other = swap(jnp.where(data == 0, part[rows:], part[:rows]), ("dp",))
    return jnp.where(
        data == 0, jnp.concatenate([own, other], axis=1), jnp.concatenate([other, own], axis=1)
    ).astype(BF)


def dot(left, right, dims):
    return lax.dot_general(left, right, (dims, ((), ())), preferred_element_type=F32)


def per_device(
    tokens, routes, route_gates, cotangent, dense_gate, dense_up, dense_down,
    expert_gate, expert_up, expert_down,
):
    width = expert_gate.shape[2]
    hidden = expert_gate.shape[1]
    data, near, core = (lax.axis_index(name) for name in ("dp", "xlo", "core"))
    rows = tokens.shape[0]
    depth = lax.axis_size("z")

    ids = jnp.arange(128, dtype=jnp.int32)
    weights_of = jnp.sum(
        jnp.where(routes[:, :, None] == ids[None, None, :], route_gates.astype(F32)[:, :, None], 0.0), axis=1
    ).astype(BF)
    marks = join([weights_of, jnp.zeros_like(weights_of)])

    def columns(at):
        both = lax.dynamic_slice_in_dim(join([tokens, cotangent]), at * width, width, axis=1)
        return jnp.concatenate([both, marks], axis=1)

    own, far = columns(data), swap(columns(1 - data), ("dp",))
    block = join([in_order(data, own[:rows], far[:rows]), in_order(data, own[rows:], far[rows:])])
    block = gather(block, "z").reshape(depth, 4 * rows, -1)

    gate, up, down = expert_gate[0], expert_up[0], expert_down[0]
    units = -(-5 * hidden // 128) * 128
    _, gate = lax.optimization_barrier((far, gate))
    gate_x = swap(gate, ("xlo",))

    def columns_of(dense):
        return lax.dynamic_slice_in_dim(dense, data * width, width, axis=1)

    def place_near(buffer, mine, dense, at):
        buffer = place(buffer, mine, at)
        buffer = place(buffer, swap(mine, ("core",)), at + 2 * hidden)
        return place(buffer, columns_of(dense), at + 4 * hidden)

    def place_far(buffer, theirs, at):
        buffer = place(buffer, theirs, at + hidden)
        return place(buffer, swap(theirs, ("core",)), at + 3 * hidden)

    pair = jnp.zeros((2 * units, width), BF)
    pair = place_near(place_near(pair, gate, dense_gate, 0), up, dense_up, units)
    up_late, _, _ = lax.optimization_barrier((up, gate_x, pair))
    up_x = swap(up_late, ("xlo",))
    down_late, _ = lax.optimization_barrier((down, up_x))
    down_x = swap(down_late, ("xlo",))

    block, pair, down = lax.optimization_barrier((block, pair, down))
    tok = gather(block[:, :2 * rows].reshape(-1, block.shape[2]), "y").reshape(-1, block.shape[2])
    last = place_near(jnp.zeros((units, width), BF), down, dense_down, 0)
    pair = place_far(pair, gate_x, 0)
    block, tok, pair, last = lax.optimization_barrier((block, tok, pair, last))
    cot = gather(block[:, 2 * rows:, :width].reshape(-1, width), "y").reshape(-1, width)
    pair = place_far(pair, up_x, units)

    weighting = tok[:, width:].astype(F32)
    tok = tok[:, :width]

    unit = jnp.arange(units, dtype=jnp.int32)[None]
    scale = jnp.ones((), F32)
    for at, chip, other in ((0, near, core), (1, 1 - near, core), (2, near, 1 - core), (3, 1 - near, 1 - core)):
        column = jnp.sum(
            jnp.where(ids[None] == chip * lax.axis_size("core") + other, weighting, 0.0), axis=1, keepdims=True
        )
        scale = jnp.where((unit >= at * hidden) & (unit < (at + 1) * hidden), column, scale)

    both = dot(tok, pair, ((1,), (1,))).astype(BF)
    both, down_x, cot = lax.optimization_barrier((both, down_x, cot))
    last = place_far(last, down_x, 0)
    dact = dot(cot, last, ((1,), (1,))).astype(BF)
    far_both, _ = lax.optimization_barrier((swap(both, ("dp",)), dact))
    both = both.astype(F32) + far_both.astype(F32)
    dact = dact.astype(F32) + swap(dact, ("dp",)).astype(F32)
    pre, lin = both[:, :units], both[:, units:]
    sig = jax.nn.sigmoid(pre)
    act = (pre * sig * lin * scale).astype(BF)
    gate_slope = lin * scale * (sig * (1.0 + pre * (1.0 - sig)))
    lin_slope = pre * sig * scale
    mixed = dot(act, last, ((1,), (0,))).astype(BF)

    def far_grads(left, right):
        ours = dot(left[:, :2 * hidden], right, ((0,), (0,))).astype(BF)
        theirs = swap(dot(left[:, 2 * hidden:4 * hidden], right, ((0,), (0,))).astype(BF), ("core",))
        return ours, theirs, (ours[hidden:].astype(F32) + theirs[hidden:].astype(F32)).astype(BF)

    def whole_grad(ours, theirs, far):
        return (ours[:hidden].astype(F32) + theirs[:hidden].astype(F32) + far.astype(F32)).astype(BF)[None]

    down_ours, down_theirs, down_far = far_grads(act, cot)
    mixed, down_far = lax.optimization_barrier((mixed, down_far))
    dact, _ = lax.optimization_barrier((dact, mixed))
    down_far = swap(down_far, ("xlo",))
    mixed = scatter(mixed, "y").astype(BF)
    slopes = jnp.concatenate([dact * gate_slope, dact * lin_slope], axis=1).astype(BF)
    grads = dot(slopes, pair, ((1,), (0,))).astype(BF)
    gate_ours, gate_theirs, gate_far = far_grads(slopes[:, :units], tok)
    grads, gate_far, mixed, down_far = lax.optimization_barrier((grads, gate_far, mixed, down_far))
    gate_far = swap(gate_far, ("xlo",))
    grads = scatter(grads, "y").astype(BF)
    up_ours, up_theirs, up_far = far_grads(slopes[:, units:], tok)
    both = jnp.concatenate([part.reshape(depth, 2 * rows, width) for part in (mixed, grads)], axis=1)
    both, up_far, gate_far = lax.optimization_barrier((both, up_far, gate_far))
    up_far = swap(up_far, ("xlo",))
    both = scatter(both.reshape(-1, width), "z")
    mixed, grads = finish(both[:2 * rows], data), finish(both[2 * rows:], data)
    return (
        mixed,
        grads,
        whole_grad(gate_ours, gate_theirs, gate_far),
        whole_grad(up_ours, up_theirs, up_far),
        whole_grad(down_ours, down_theirs, down_far),
    )


def solution(mesh):
    fine = Mesh(mesh.devices.reshape(2, 2, 2, 8, 4), ("dp", "xlo", "core", "z", "y"))
    every = ("dp", "xlo", "core", "z", "y")
    row = P(every, None)
    dense = P(("z", "y"), None)
    expert = P(("xlo", "core"), ("z", "y"), "dp")
    return jax.shard_map(
        per_device,
        mesh=fine,
        in_specs=(row, row, row, row, dense, dense, dense, expert, expert, expert),
        out_specs=(row, row, expert, expert, expert),
        check_vma=False,
    )
```
